512 devices in a mesh: row: 32 (over z, x), col: 16 (over y, core).
Axes of the slice: x: 4, y: 8, z: 8, core: 2. Of those that a mesh axis runs over, the one named last changes fastest.
Arguments:
- hamiltonian: float32 [24576, 24576], P('row', 'col'), may hold values from -1 to 4, as said below
- search_block: float32 [24576, 256], P(('col', 'row')), may hold values from -6 to 6
- filter_bounds: float32 [3], replicated, may hold values from -2 to 6, as said below
Outputs:
- first_filtered: float32 [24576, 256], P(('row', 'col'))
- second_filtered: float32 [24576, 256], P(('col', 'row'))
The draws below stay inside these ranges and needn't reach their ends.
Inputs may be any that keep to these rules, and one draw needn't show every extreme that they name: `hamiltonian`: symmetric; its diagonal dominates each entry off it. `filter_bounds`: increasing: lower < low_end < high_end, lower below the spectrum and high_end above it.
All inputs are finite; a program needn't handle non-finite values.
Results may differ from the reference program's by a relative error of at most 0.000092.
Values sent between devices are 32-bit elements; how exact they have to be, the bound alone decides.
No kernel may reach another device: no remote copies, remote signals or barrier semaphores. Data moves between devices by JAX's collectives and lax.ppermute only.
A program may use at most 64 MiB of HBM per device.

```python
import math
import jax
import jax.numpy as jnp
from jax import lax

N = 24576
K = 256


def draw_hamiltonian(key, part):
    key = jax.random.fold_in(key, 11)
    first_key, second_key = jax.random.split(key)
    noise = jax.random.normal(first_key, (N, N), jnp.float32)
    energies = jax.random.uniform(second_key, (N,), jnp.float32, 1.0, 3.0)
    coupling = (noise + noise.T) * (0.5 / math.sqrt(N))
    indices = jnp.arange(N, dtype=jnp.int32)
    return jnp.where(indices[:, None] == indices[None, :], energies[:, None], coupling)


def draw_filter_bounds(key, part):
    key = jax.random.fold_in(key, 23)
    values = jax.random.uniform(key, (3,), jnp.float32, 0.0, 1.0)
    return jnp.stack([values[0] - 2.0, values[1] + 1.5, values[2] + 5.0])


def block_scale(rng, shape, cuts, low, top_value):
    loudness = 1.0
    for dim, shards_of in cuts:
        heights = jax.random.uniform(jax.random.fold_in(jax.random.fold_in(rng, 6), dim), (shards_of,), jnp.float32, low / len(cuts), top_value / len(cuts))
        loudness = loudness * jnp.repeat(jnp.exp(heights), shape[dim] // shards_of).reshape((-1,) + (1,) * (len(shape) - 1 - dim))
    return loudness


def gaussian(stream_key, extent, spread, most, cuts=(), kind=jnp.bfloat16):
    result = spread * jax.random.normal(stream_key, extent, jnp.float32)
    if cuts:
        result = result * block_scale(stream_key, extent, cuts, -0.22, 0.18)
    return jnp.clip(result, -most, most).astype(kind)


def setup_inputs(seed: int = 0) -> dict:
    keys = jax.random.split(jax.random.key(seed), 4)
    return {
        "hamiltonian": draw_hamiltonian(jax.random.fold_in(keys[3], 71), 0),
        "search_block": gaussian(keys[1], (N, K), 1.0, 6.0, ((0, 512),), jnp.float32),
        "filter_bounds": draw_filter_bounds(jax.random.fold_in(keys[3], 71), 0),
    }


def reference(hamiltonian, search_block, filter_bounds):
    lower = filter_bounds[0]
    low_end = filter_bounds[1]
    high_end = filter_bounds[2]
    center = (high_end + low_end) / 2.0
    half = (high_end - low_end) / 2.0
    sigma_one = half / (lower - center)
    sigma_two = 1.0 / (2.0 / sigma_one - sigma_one)
    scale_one = sigma_one / half
    scale_two = 2.0 * sigma_two / half
    damp = sigma_two * sigma_one
    shifted = hamiltonian - center * jnp.eye(N, dtype=jnp.float32)
    first = scale_one * jnp.dot(shifted, search_block, preferred_element_type=jnp.float32, precision=lax.Precision.HIGHEST)
    second = scale_two * jnp.dot(shifted, first, preferred_element_type=jnp.float32, precision=lax.Precision.HIGHEST) - damp * search_block
    return first, second
```

```python
import jax
import jax.numpy as jnp
from jax import lax
from jax.sharding import Mesh, PartitionSpec as P


def body(hamiltonian, search_block, filter_bounds):
    lower = filter_bounds[0]
    low_end = filter_bounds[1]
    high_end = filter_bounds[2]
    center = (high_end + low_end) / 2.0
    half = (high_end - low_end) / 2.0
    sigma_one = half / (lower - center)
    sigma_two = 1.0 / (2.0 / sigma_one - sigma_one)
    scale_one = sigma_one / half
    scale_two = 2.0 * sigma_two / half
    damp = sigma_two * sigma_one

    zs, xs, ys, cs = (lax.axis_size(a) for a in ("z", "x", "y", "c"))
    z, x, y, c = (lax.axis_index(a) for a in ("z", "x", "y", "c"))
    rows_tile, cols_tile = hamiltonian.shape
    piece, width = search_block.shape
    part = width // cs
    swap = [(i, cs - 1 - i) for i in range(cs)]

    other = lax.ppermute(hamiltonian, "c", swap)
    global_rows = (z * xs + x) * rows_tile + jnp.arange(rows_tile, dtype=jnp.int32)[:, None]

    def shift(tile, core):
        global_cols = (y * cs + core) * cols_tile + jnp.arange(cols_tile, dtype=jnp.int32)[None, :]
        return tile - center * (global_rows == global_cols).astype(jnp.float32)

    mine = shift(hamiltonian, c)
    theirs = shift(other, cs - 1 - c)

    halves = search_block.reshape(piece, cs, part).transpose(1, 0, 2)
    sent = jnp.broadcast_to(halves[None], (zs, cs, piece, part)).reshape(zs * cs, piece, part)
    got = lax.all_to_all(sent, ("z", "c"), 0, 0, tiled=True)
    sent = jnp.broadcast_to(got[None], (xs,) + got.shape)
    got = lax.all_to_all(sent, "x", 0, 0, tiled=True)
    got = got.reshape(xs, zs, cs, piece, part).transpose(2, 1, 0, 3, 4).reshape(cs, cols_tile, part)
    got_mine = lax.dynamic_index_in_dim(got, c, 0, keepdims=False)
    got_theirs = lax.dynamic_index_in_dim(got, cs - 1 - c, 0, keepdims=False)

    def dot(a, b, dims):
        return lax.dot_general(
            a, b, (dims, ((), ())), precision=lax.Precision.HIGH, preferred_element_type=jnp.float32
        )

    partial_rows = dot(mine, got_mine, ((1,), (0,))) + dot(theirs, got_theirs, ((1,), (0,)))
    share = rows_tile // ys
    terms = lax.all_to_all(partial_rows.reshape(ys, share, part), "y", 0, 0, tiled=True)
    first = scale_one * terms.sum(0)
    sent = jnp.broadcast_to(first[None], (ys, share, part))
    first_rows = lax.all_to_all(sent, "y", 0, 0, tiled=True).reshape(rows_tile, part)

    first_pair = first.reshape(cs, piece, part)
    keep = lax.dynamic_index_in_dim(first_pair, c, 0, keepdims=False)
    give = lax.dynamic_index_in_dim(first_pair, cs - 1 - c, 0, keepdims=False)
    came = lax.ppermute(give, "c", swap)
    first_out = jnp.where(c == 0, jnp.concatenate([keep, came], 1), jnp.concatenate([came, keep], 1))

    out_mine = dot(mine, first_rows, ((0,), (0,)))
    out_theirs = dot(theirs, first_rows, ((0,), (0,)))
    both = jnp.where(c == 0, jnp.stack([out_mine, out_theirs]), jnp.stack([out_theirs, out_mine]))
    sent = both.reshape(cs, zs, xs, piece, part).transpose(2, 1, 0, 3, 4).reshape(xs, zs * cs, piece, part)
    summed = lax.all_to_all(sent, "x", 0, 0, tiled=True).sum(0)
    summed = lax.all_to_all(summed, ("z", "c"), 0, 0, tiled=True)
    summed = summed.reshape(zs, cs, piece, part).sum(0).transpose(1, 0, 2).reshape(piece, width)
    second_out = scale_two * summed - damp * search_block
    return (first_out, second_out)


def solution(mesh):
    fine = Mesh(mesh.devices.reshape(8, 4, 8, 2), ("z", "x", "y", "c"))
    row, col = ("z", "x"), ("y", "c")
    return jax.shard_map(
        body,
        mesh=fine,
        in_specs=(P(row, col), P(col + row, None), P()),
        out_specs=(P(row + col, None), P(col + row, None)),
        check_vma=False,
    )
```

```python
import jax
import jax.numpy as jnp
from jax import lax
from jax.experimental import pallas as pl
from jax.experimental.pallas import tpu as pltpu
from jax.sharding import Mesh, PartitionSpec as P

BF, F32 = jnp.bfloat16, jnp.float32
VMEM_LIMIT = 16 * 1024 * 1024


def split(v):
    hi = v.astype(BF)
    return hi, (v - hi.astype(F32)).astype(BF)


def split_kernel(place_ref, center_ref, mine_ref, theirs_ref, out_ref):
    rows, cols = mine_ref.shape
    core = place_ref[0]
    first_row = place_ref[1] + pl.program_id(0) * rows
    row = lax.broadcasted_iota(jnp.int32, (rows, cols), 0)
    col = lax.broadcasted_iota(jnp.int32, (rows, cols), 1)
    center = center_ref[0]
    for block, tile_ref in ((core, mine_ref), (1 - core, theirs_ref)):
        first_col = place_ref[2] + block * cols
        tile = tile_ref[...] - jnp.where(row + (first_row - first_col) == col, center, 0.0)
        hi, lo = split(tile)
        out_ref[block, 0] = hi
        out_ref[block, 1] = lo


def split_tiles(place, center, mine, theirs, step=128):
    rows, cols = mine.shape
    smem = pl.BlockSpec(memory_space=pltpu.SMEM)
    tile = pl.BlockSpec((step, cols), lambda i: (i, 0))
    return pl.pallas_call(
        split_kernel,
        grid=(rows // step,),
        in_specs=[smem, smem, tile, tile],
        out_specs=pl.BlockSpec((2, 2, step, cols), lambda i: (0, 0, i, 0)),
        out_shape=jax.ShapeDtypeStruct((2, 2, rows, cols), BF),
        compiler_params=pltpu.CompilerParams(vmem_limit_bytes=VMEM_LIMIT),
        cost_estimate=pl.CostEstimate(flops=8 * rows * cols, bytes_accessed=16 * rows * cols, transcendentals=0),
    )(place, center, mine, theirs)


def rows_kernel(h_ref, x_ref, out_ref, wide):
    xs, zc, piece, part = x_ref.shape

    @pl.when(pl.program_id(0) == 0)
    def _():
        for zi in range(zc // 2):
            for block in range(2):
                for xi in range(xs):
                    hi, lo = split(x_ref[xi, zi * 2 + block])
                    at = pl.ds((zi * xs + xi) * piece, piece)
                    wide[block, at, :part] = hi
                    wide[block, at, part:] = lo

    step, cols = h_ref.shape[2:]
    acc = jnp.dot(h_ref[0].reshape(2 * step, cols), wide[0], preferred_element_type=F32)
    acc += jnp.dot(h_ref[1].reshape(2 * step, cols), wide[1], preferred_element_type=F32)
    acc = acc[:, :part] + acc[:, part:]
    out_ref[...] = acc[:step] + acc[step:]


def rows_product(h, x, step=128):
    _, _, rows, cols = h.shape
    xs, zc, piece, part = x.shape
    return pl.pallas_call(
        rows_kernel,
        grid=(rows // step,),
        in_specs=[
            pl.BlockSpec((2, 2, step, cols), lambda i: (0, 0, i, 0)),
            pl.BlockSpec(x.shape, lambda i: (0, 0, 0, 0)),
        ],
        out_specs=pl.BlockSpec((step, part), lambda i: (i, 0)),
        out_shape=jax.ShapeDtypeStruct((rows, part), F32),
        scratch_shapes=[pltpu.VMEM((2, cols, 2 * part), BF)],
        compiler_params=pltpu.CompilerParams(vmem_limit_bytes=VMEM_LIMIT),
        cost_estimate=pl.CostEstimate(
            flops=16 * rows * cols * part, bytes_accessed=8 * rows * cols, transcendentals=0
        ),
    )(h, x)


def cols_kernel(h_ref, y_ref, out_ref, tall):
    xs, zs, _, piece, part = out_ref.shape

    @pl.when((pl.program_id(0) == 0) & (pl.program_id(1) == 0))
    def _():
        share = y_ref.shape[1]
        flat = y_ref[...].reshape(y_ref.shape[0] * share, part).T
        hi, lo = split(flat)
        tall[:part] = hi
        tall[part:] = lo

    acc = jnp.dot(tall[...], h_ref[0, 0], preferred_element_type=F32)
    acc += jnp.dot(tall[...], h_ref[0, 1], preferred_element_type=F32)
    out = (acc[:part] + acc[part:]).T
    for zi in range(zs):
        for xi in range(xs):
            at = (zi * xs + xi) * piece
            out_ref[xi, zi, 0] = out[at : at + piece]


def cols_product(h, y, xs, zs, steps=2):
    _, _, rows, cols = h.shape
    part = y.shape[-1]
    piece = cols // (xs * zs)
    return pl.pallas_call(
        cols_kernel,
        grid=(2, steps),
        in_specs=[
            pl.BlockSpec((1, 2, rows, cols // steps), lambda b, j: (b, 0, 0, j)),
            pl.BlockSpec(y.shape, lambda b, j: (0, 0, 0)),
        ],
        out_specs=pl.BlockSpec((xs, zs // steps, 1, piece, part), lambda b, j: (0, j, b, 0, 0)),
        out_shape=jax.ShapeDtypeStruct((xs, zs, 2, piece, part), F32),
        scratch_shapes=[pltpu.VMEM((2 * part, rows), BF)],
        compiler_params=pltpu.CompilerParams(vmem_limit_bytes=VMEM_LIMIT),
        cost_estimate=pl.CostEstimate(
            flops=16 * rows * cols * part, bytes_accessed=8 * rows * cols, transcendentals=0
        ),
    )(h, y)


def body(hamiltonian, search_block, filter_bounds):
    lower = filter_bounds[0]
    low_end = filter_bounds[1]
    high_end = filter_bounds[2]
    center = (high_end + low_end) / 2.0
    half = (high_end - low_end) / 2.0
    sigma_one = half / (lower - center)
    sigma_two = 1.0 / (2.0 / sigma_one - sigma_one)
    scale_one = sigma_one / half
    scale_two = 2.0 * sigma_two / half
    damp = sigma_two * sigma_one

    zs, xs, ys, cs = (lax.axis_size(a) for a in ("z", "x", "y", "c"))
    z, x, y, c = (lax.axis_index(a) for a in ("z", "x", "y", "c"))
    rows_tile, cols_tile = hamiltonian.shape
    piece, width = search_block.shape
    part = width // cs
    swap = [(i, cs - 1 - i) for i in range(cs)]

    other = lax.ppermute(hamiltonian, "c", swap)
    place = jnp.stack([c, (z * xs + x) * rows_tile, y * cs * cols_tile]).astype(jnp.int32)
    tiles = split_tiles(place, center.reshape(1), hamiltonian, other)

    halves = search_block.reshape(piece, cs, part).transpose(1, 0, 2)
    sent = jnp.broadcast_to(halves[None], (zs, cs, piece, part)).reshape(zs * cs, piece, part)
    got = lax.all_to_all(sent, ("z", "c"), 0, 0, tiled=True)
    sent = jnp.broadcast_to(got[None], (xs,) + got.shape)
    got = lax.all_to_all(sent, "x", 0, 0, tiled=True)

    partial_rows = rows_product(tiles, got)
    share = rows_tile // ys
    terms = lax.all_to_all(partial_rows.reshape(ys, share, part), "y", 0, 0, tiled=True)
    first = scale_one * terms.sum(0)
    sent = jnp.broadcast_to(first[None], (ys, share, part))
    first_rows = lax.all_to_all(sent, "y", 0, 0, tiled=True)

    first_pair = first.reshape(cs, piece, part)
    keep = lax.dynamic_index_in_dim(first_pair, c, 0, keepdims=False)
    give = lax.dynamic_index_in_dim(first_pair, cs - 1 - c, 0, keepdims=False)
    came = lax.ppermute(give, "c", swap)
    first_out = jnp.where(c == 0, jnp.concatenate([keep, came], 1), jnp.concatenate([came, keep], 1))

    sent = cols_product(tiles, first_rows, xs, zs).reshape(xs, zs * cs, piece, part)
    summed = lax.all_to_all(sent, "x", 0, 0, tiled=True).sum(0)
    summed = lax.all_to_all(summed, ("z", "c"), 0, 0, tiled=True)
    summed = summed.reshape(zs, cs, piece, part).sum(0).transpose(1, 0, 2).reshape(piece, width)
    second_out = scale_two * summed - damp * search_block
    return (first_out, second_out)


def solution(mesh):
    fine = Mesh(mesh.devices.reshape(8, 4, 8, 2), ("z", "x", "y", "c"))
    row, col = ("z", "x"), ("y", "c")
    return jax.shard_map(
        body,
        mesh=fine,
        in_specs=(P(row, col), P(col + row, None), P()),
        out_specs=(P(row + col, None), P(col + row, None)),
        check_vma=False,
    )
```

```python
import jax
import jax.numpy as jnp
from jax import lax
from jax.experimental import pallas as pl
from jax.experimental.pallas import tpu as pltpu
from jax.sharding import Mesh, PartitionSpec as P

BF, F32 = jnp.bfloat16, jnp.float32
SMEM = pl.BlockSpec(memory_space=pltpu.SMEM)
VMEM = pl.BlockSpec(memory_space=pltpu.VMEM)
HBM = pl.BlockSpec(memory_space=pl.ANY)
AHEAD = 3
PARAMS = pltpu.CompilerParams(vmem_limit_bytes=60 * 1024 * 1024)


def split(v):
    hi = v.astype(BF)
    return hi, (v - hi.astype(F32)).astype(BF)


def deal_kernel(search_ref, out_ref):
    part = out_ref.shape[-1]
    for zi in range(out_ref.shape[0]):
        for ci in range(out_ref.shape[1]):
            out_ref[zi, ci] = search_ref[:, ci * part : (ci + 1) * part]


def split_kernel(place_ref, bounds_ref, mine_ref, theirs_ref, mine_out, theirs_out, scalars_ref):
    rows, cols = mine_ref.shape
    center = (bounds_ref[2] + bounds_ref[1]) / 2.0
    row = lax.broadcasted_iota(jnp.int32, (rows, cols), 0)
    col = lax.broadcasted_iota(jnp.int32, (rows, cols), 1)
    apart = col - row
    for t, (tile_ref, out_ref) in enumerate(((mine_ref, mine_out), (theirs_ref, theirs_out))):
        offset = place_ref[t] + pl.program_id(0) * rows
        hi, lo = split(tile_ref[...] - jnp.where(apart == offset, center, 0.0))
        out_ref[0] = hi
        out_ref[1] = lo

    @pl.when(pl.program_id(0) == 0)
    def _():
        lower, low_end, high_end = (jnp.full((1, scalars_ref.shape[1]), bounds_ref[i], F32) for i in range(3))
        center = (high_end + low_end) / 2.0
        half = (high_end - low_end) / 2.0
        sigma_one = half / (lower - center)
        sigma_two = 1.0 / (2.0 / sigma_one - sigma_one)
        scalars_ref[0:1] = sigma_one / half
        scalars_ref[1:2] = 2.0 * sigma_two / half
        scalars_ref[2:3] = sigma_two * sigma_one


def split_tiles(offsets, bounds, mine, theirs, width, step=256):
    rows, cols = mine.shape
    tile = pl.BlockSpec((step, cols), lambda i: (i, 0))
    out = pl.BlockSpec((2, step, cols), lambda i: (0, i, 0))
    return pl.pallas_call(
        split_kernel,
        grid=(rows // step,),
        in_specs=[SMEM, SMEM, tile, tile],
        out_specs=(out, out, pl.BlockSpec((8, width), lambda i: (0, 0))),
        out_shape=(
            jax.ShapeDtypeStruct((2, rows, cols), BF),
            jax.ShapeDtypeStruct((2, rows, cols), BF),
            jax.ShapeDtypeStruct((8, width), F32),
        ),
        compiler_params=PARAMS,
        cost_estimate=pl.CostEstimate(flops=16 * rows * cols, bytes_accessed=16 * rows * cols, transcendentals=0),
    )(offsets, bounds, mine, theirs)


def stream(copies, ahead):
    for copy in copies[:ahead]:
        copy.start()
    yield
    for i, copy in enumerate(copies):
        copy.wait()
        if i + ahead < len(copies):
            copies[i + ahead].start()
        yield


def rows_kernel(core_ref, mine_ref, theirs_ref, x_ref, out_ref, tiles, wide, sems):
    outer, inner, piece, part = x_ref.shape
    steps, step, cols = tiles.shape[1], tiles.shape[3], tiles.shape[4]
    landed = stream(
        [
            pltpu.make_async_copy(ref.at[:, pl.ds(i * step, step), :], tiles.at[t, i], sems.at[t, i])
            for i in range(steps)
            for t, ref in enumerate((mine_ref, theirs_ref))
        ],
        AHEAD,
    )
    next(landed)
    for t in range(2):
        block = core_ref[0] if t == 0 else 1 - core_ref[0]
        for zi in range(inner // 2):
            for xi in range(outer):
                hi, lo = split(x_ref[xi, zi * 2 + block])
                at = pl.ds((zi * outer + xi) * piece, piece)
                wide[t, at, :part] = hi
                wide[t, at, part:] = lo
    for i in range(steps):
        acc = None
        for t in range(2):
            next(landed)
            term = jnp.dot(tiles[t, i].reshape(2 * step, cols), wide[t], preferred_element_type=F32)
            acc = term if acc is None else acc + term
        acc = acc[:, :part] + acc[:, part:]
        out_ref[pl.ds(i * step, step), :] = acc[:step] + acc[step:]


def rows_product(core, mine, theirs, x, step=256):
    _, rows, cols = mine.shape
    part = x.shape[-1]
    return pl.pallas_call(
        rows_kernel,
        in_specs=[SMEM, HBM, HBM, VMEM],
        out_specs=VMEM,
        out_shape=jax.ShapeDtypeStruct((rows, part), F32),
        scratch_shapes=[
            pltpu.VMEM((2, rows // step, 2, step, cols), BF),
            pltpu.VMEM((2, cols, 2 * part), BF),
            pltpu.SemaphoreType.DMA((2, rows // step)),
        ],
        compiler_params=PARAMS,
        cost_estimate=pl.CostEstimate(
            flops=16 * rows * cols * part, bytes_accessed=8 * rows * cols, transcendentals=0
        ),
    )(core, mine, theirs, x)


def cols_kernel(core_ref, mine_ref, theirs_ref, y_ref, out_ref, tiles, tall, sems):
    outer, _, piece, part = out_ref.shape
    steps, depths, depth, step = tiles.shape[1], tiles.shape[2], tiles.shape[4], tiles.shape[5]
    landed = stream(
        [
            pltpu.make_async_copy(
                ref.at[:, pl.ds(k * depth, depth), pl.ds(i * step, step)], tiles.at[t, i, k], sems.at[t, i, k]
            )
            for i in range(steps)
            for t, ref in enumerate((mine_ref, theirs_ref))
            for k in range(depths)
        ],
        AHEAD,
    )
    next(landed)
    hi, lo = split(y_ref[...].reshape(-1, part).T)
    tall[:part] = hi
    tall[part:] = lo
    for i in range(steps):
        for t in range(2):
            block = core_ref[0] if t == 0 else 1 - core_ref[0]
            acc = None
            for k in range(depths):
                next(landed)
                for half in range(2):
                    term = jnp.dot(
                        tall[:, k * depth : (k + 1) * depth], tiles[t, i, k, half], preferred_element_type=F32
                    )
                    acc = term if acc is None else acc + term
            out = (acc[:part] + acc[part:]).T
            for p in range(step // piece):
                zi, xi = divmod(i * (step // piece) + p, outer)
                out_ref[xi, zi * 2 + block] = out[p * piece : (p + 1) * piece]


def cols_product(core, mine, theirs, y, outer, piece, step=768, depth=384):
    _, rows, cols = mine.shape
    part = y.shape[-1]
    return pl.pallas_call(
        cols_kernel,
        in_specs=[SMEM, HBM, HBM, VMEM],
        out_specs=VMEM,
        out_shape=jax.ShapeDtypeStruct((outer, 2 * cols // (outer * piece), piece, part), F32),
        scratch_shapes=[
            pltpu.VMEM((2, cols // step, rows // depth, 2, depth, step), BF),
            pltpu.VMEM((2 * part, rows), BF),
            pltpu.SemaphoreType.DMA((2, cols // step, rows // depth)),
        ],
        compiler_params=PARAMS,
        cost_estimate=pl.CostEstimate(
            flops=16 * rows * cols * part, bytes_accessed=8 * rows * cols, transcendentals=0
        ),
    )(core, mine, theirs, y)


def body(hamiltonian, search_block, filter_bounds):
    z2s, z1s, xs, ys, cs = (lax.axis_size(a) for a in ("z2", "z1", "x", "y", "c"))
    z2, z1, x, y, c = (lax.axis_index(a) for a in ("z2", "z1", "x", "y", "c"))
    rows_tile, cols_tile = hamiltonian.shape
    piece, width = search_block.shape
    part = width // cs
    outer = z1s * xs
    swap = [(i, cs - 1 - i) for i in range(cs)]
    core = c.reshape(1).astype(jnp.int32)

    first_row = ((z2 * z1s + z1) * xs + x) * rows_tile
    first_col = y * cs * cols_tile
    other = lax.ppermute(hamiltonian, "c", swap)
    offsets = (first_row - first_col - jnp.stack([c, cs - 1 - c]) * cols_tile).astype(jnp.int32)
    mine, theirs, scalars = split_tiles(offsets, filter_bounds, hamiltonian, other, width)

    sent = pl.pallas_call(deal_kernel, out_shape=jax.ShapeDtypeStruct((z2s, cs, piece, part), F32))(search_block)
    got = lax.all_to_all(sent.reshape(z2s * cs, piece, part), ("z2", "c"), 0, 0, tiled=True)
    got, mine, theirs, scalars = lax.optimization_barrier((got, mine, theirs, scalars))
    scale_one, scale_two, damp = scalars[0, :part], scalars[1, :part], scalars[2]
    sent = jnp.broadcast_to(got[None], (outer,) + got.shape)
    got = lax.all_to_all(sent, ("z1", "x"), 0, 0, tiled=True)

    partial_rows = rows_product(core, mine, theirs, got)
    share = rows_tile // ys
    terms = lax.all_to_all(partial_rows.reshape(ys, share, part), "y", 0, 0, tiled=True)
    first = scale_one * terms.sum(0)
    sent = jnp.broadcast_to(first[None], terms.shape)
    first_rows = lax.all_to_all(sent, "y", 0, 0, tiled=True)

    first_pair = first.reshape(cs, piece, part)
    keep = lax.dynamic_index_in_dim(first_pair, c, 0, keepdims=False)
    give = lax.dynamic_index_in_dim(first_pair, cs - 1 - c, 0, keepdims=False)
    came = lax.ppermute(give, "c", swap)
    first_out = jnp.where(c == 0, jnp.concatenate([keep, came], 1), jnp.concatenate([came, keep], 1))

    sent = cols_product(core, mine, theirs, first_rows, outer, piece)
    summed = lax.all_to_all(sent, ("z1", "x"), 0, 0, tiled=True).sum(0)
    summed = lax.all_to_all(summed, ("z2", "c"), 0, 0, tiled=True)
    summed = scale_two * summed.reshape(z2s, cs, piece, part).sum(0)
    second_out = summed.transpose(1, 0, 2).reshape(piece, width) - damp * search_block
    return (first_out, second_out)


def solution(mesh):
    fine = Mesh(mesh.devices.reshape(4, 2, 4, 8, 2), ("z2", "z1", "x", "y", "c"))
    row, col = ("z2", "z1", "x"), ("y", "c")
    return jax.shard_map(
        body,
        mesh=fine,
        in_specs=(P(row, col), P(col + row, None), P()),
        out_specs=(P(row + col, None), P(col + row, None)),
        check_vma=False,
    )
```

```python
import jax
import jax.numpy as jnp
from jax import lax
from jax.experimental import pallas as pl
from jax.experimental.pallas import tpu as pltpu
from jax.sharding import Mesh, PartitionSpec as P

BF, F32 = jnp.bfloat16, jnp.float32
SMEM = pl.BlockSpec(memory_space=pltpu.SMEM)
PARAMS = pltpu.CompilerParams(vmem_limit_bytes=60 * 1024 * 1024)


def split(v):
    hi = v.astype(BF)
    return hi, (v - hi.astype(F32)).astype(BF)


def deal_kernel(search_ref, out_ref):
    part = out_ref.shape[-1]
    for zi in range(out_ref.shape[0]):
        for ci in range(out_ref.shape[1]):
            out_ref[zi, ci] = search_ref[:, ci * part : (ci + 1) * part]


def split_kernel(place_ref, bounds_ref, mine_ref, theirs_ref, out_ref, scalars_ref):
    rows, cols = mine_ref.shape
    core = place_ref[0]
    center = (bounds_ref[2] + bounds_ref[1]) / 2.0
    row = lax.broadcasted_iota(jnp.int32, (rows, cols), 0)
    col = lax.broadcasted_iota(jnp.int32, (rows, cols), 1)
    apart = col - row
    for block, tile_ref in ((core, mine_ref), (1 - core, theirs_ref)):
        offset = place_ref[1] + pl.program_id(0) * rows - block * cols
        hi, lo = split(tile_ref[...] - jnp.where(apart == offset, center, 0.0))
        out_ref[block, 0] = hi
        out_ref[block, 1] = lo

    @pl.when(pl.program_id(0) == 0)
    def _():
        lower, low_end, high_end = (jnp.full((1, scalars_ref.shape[1]), bounds_ref[i], F32) for i in range(3))
        center = (high_end + low_end) / 2.0
        half = (high_end - low_end) / 2.0
        sigma_one = half / (lower - center)
        sigma_two = 1.0 / (2.0 / sigma_one - sigma_one)
        scalars_ref[0:1] = sigma_one / half
        scalars_ref[1:2] = 2.0 * sigma_two / half
        scalars_ref[2:3] = sigma_two * sigma_one


def split_tiles(place, bounds, mine, theirs, width, step=128):
    rows, cols = mine.shape
    tile = pl.BlockSpec((step, cols), lambda i: (i, 0))
    out = pl.BlockSpec((2, 2, step, cols), lambda i: (0, 0, i, 0))
    return pl.pallas_call(
        split_kernel,
        grid=(rows // step,),
        in_specs=[SMEM, SMEM, tile, tile],
        out_specs=(out, pl.BlockSpec((8, width), lambda i: (0, 0))),
        out_shape=(
            jax.ShapeDtypeStruct((2, 2, rows, cols), BF),
            jax.ShapeDtypeStruct((8, width), F32),
        ),
        compiler_params=PARAMS,
        cost_estimate=pl.CostEstimate(flops=16 * rows * cols, bytes_accessed=16 * rows * cols, transcendentals=0),
    )(place, bounds, mine, theirs)


def rows_kernel(h_ref, x_ref, out_ref, wide):
    xs, zc, piece, part = x_ref.shape

    @pl.when(pl.program_id(0) == 0)
    def _():
        for zi in range(zc // 2):
            for block in range(2):
                for xi in range(xs):
                    hi, lo = split(x_ref[xi, zi * 2 + block])
                    at = pl.ds((zi * xs + xi) * piece, piece)
                    wide[block, at, :part] = hi
                    wide[block, at, part:] = lo

    step, cols = h_ref.shape[2:]
    acc = jnp.dot(h_ref[0].reshape(2 * step, cols), wide[0], preferred_element_type=F32)
    acc += jnp.dot(h_ref[1].reshape(2 * step, cols), wide[1], preferred_element_type=F32)
    acc = acc[:, :part] + acc[:, part:]
    out_ref[...] = acc[:step] + acc[step:]


def rows_product(h, x, step=256):
    _, _, rows, cols = h.shape
    xs, zc, piece, part = x.shape
    return pl.pallas_call(
        rows_kernel,
        grid=(rows // step,),
        in_specs=[
            pl.BlockSpec((2, 2, step, cols), lambda i: (0, 0, i, 0)),
            pl.BlockSpec(x.shape, lambda i: (0, 0, 0, 0)),
        ],
        out_specs=pl.BlockSpec((step, part), lambda i: (i, 0)),
        out_shape=jax.ShapeDtypeStruct((rows, part), F32),
        scratch_shapes=[pltpu.VMEM((2, cols, 2 * part), BF)],
        compiler_params=PARAMS,
        cost_estimate=pl.CostEstimate(
            flops=16 * rows * cols * part, bytes_accessed=8 * rows * cols, transcendentals=0
        ),
    )(h, x)


def cols_kernel(h_ref, y_ref, out_ref, tall):
    xs, zs, _, piece, part = out_ref.shape

    @pl.when((pl.program_id(0) == 0) & (pl.program_id(1) == 0))
    def _():
        share = y_ref.shape[1]
        flat = y_ref[...].reshape(y_ref.shape[0] * share, part).T
        hi, lo = split(flat)
        tall[:part] = hi
        tall[part:] = lo

    acc = jnp.dot(tall[...], h_ref[0, 0], preferred_element_type=F32)
    acc += jnp.dot(tall[...], h_ref[0, 1], preferred_element_type=F32)
    out = (acc[:part] + acc[part:]).T
    for zi in range(zs):
        for xi in range(xs):
            at = (zi * xs + xi) * piece
            out_ref[xi, zi, 0] = out[at : at + piece]


def cols_product(h, y, xs, zs, steps=2):
    _, _, rows, cols = h.shape
    part = y.shape[-1]
    piece = cols // (xs * zs)
    return pl.pallas_call(
        cols_kernel,
        grid=(2, steps),
        in_specs=[
            pl.BlockSpec((1, 2, rows, cols // steps), lambda b, j: (b, 0, 0, j)),
            pl.BlockSpec(y.shape, lambda b, j: (0, 0, 0)),
        ],
        out_specs=pl.BlockSpec((xs, zs // steps, 1, piece, part), lambda b, j: (0, j, b, 0, 0)),
        out_shape=jax.ShapeDtypeStruct((xs, zs, 2, piece, part), F32),
        scratch_shapes=[pltpu.VMEM((2 * part, rows), BF)],
        compiler_params=PARAMS,
        cost_estimate=pl.CostEstimate(
            flops=16 * rows * cols * part, bytes_accessed=8 * rows * cols, transcendentals=0
        ),
    )(h, y)


def body(hamiltonian, search_block, filter_bounds):
    z2s, z1s, xs, ys, cs = (lax.axis_size(a) for a in ("z2", "z1", "x", "y", "c"))
    z2, z1, x, y, c = (lax.axis_index(a) for a in ("z2", "z1", "x", "y", "c"))
    rows_tile, cols_tile = hamiltonian.shape
    piece, width = search_block.shape
    part = width // cs
    outer = z1s * xs
    swap = [(i, cs - 1 - i) for i in range(cs)]

    first_row = ((z2 * z1s + z1) * xs + x) * rows_tile
    first_col = y * cs * cols_tile
    other = lax.ppermute(hamiltonian, "c", swap)
    place = jnp.stack([c, first_row - first_col]).astype(jnp.int32)
    tiles, scalars = split_tiles(place, filter_bounds, hamiltonian, other, width)

    sent = pl.pallas_call(deal_kernel, out_shape=jax.ShapeDtypeStruct((z2s, cs, piece, part), F32))(search_block)
    got = lax.all_to_all(sent.reshape(z2s * cs, piece, part), ("z2", "c"), 0, 0, tiled=True)
    got, tiles, scalars = lax.optimization_barrier((got, tiles, scalars))
    scale_one, scale_two, damp = scalars[0, :part], scalars[1, :part], scalars[2]
    sent = jnp.broadcast_to(got[None], (outer,) + got.shape)
    got = lax.all_to_all(sent, ("z1", "x"), 0, 0, tiled=True)

    partial_rows = rows_product(tiles, got)
    share = rows_tile // ys
    terms = lax.all_to_all(partial_rows.reshape(ys, share, part), "y", 0, 0, tiled=True)
    first = scale_one * terms.sum(0)
    sent = jnp.broadcast_to(first[None], terms.shape)
    first_rows = lax.all_to_all(sent, "y", 0, 0, tiled=True)

    first_pair = first.reshape(cs, piece, part)
    keep = lax.dynamic_index_in_dim(first_pair, c, 0, keepdims=False)
    give = lax.dynamic_index_in_dim(first_pair, cs - 1 - c, 0, keepdims=False)
    came = lax.ppermute(give, "c", swap)
    first_out = jnp.where(c == 0, jnp.concatenate([keep, came], 1), jnp.concatenate([came, keep], 1))

    sent = cols_product(tiles, first_rows, outer, z2s).reshape(outer, z2s * cs, piece, part)
    summed = lax.all_to_all(sent, ("z1", "x"), 0, 0, tiled=True).sum(0)
    summed = lax.all_to_all(summed, ("z2", "c"), 0, 0, tiled=True)
    summed = scale_two * summed.reshape(z2s, cs, piece, part).sum(0)
    second_out = summed.transpose(1, 0, 2).reshape(piece, width) - damp * search_block
    return (first_out, second_out)


def solution(mesh):
    fine = Mesh(mesh.devices.reshape(4, 2, 4, 8, 2), ("z2", "z1", "x", "y", "c"))
    row, col = ("z2", "z1", "x"), ("y", "c")
    return jax.shard_map(
        body,
        mesh=fine,
        in_specs=(P(row, col), P(col + row, None), P()),
        out_specs=(P(row + col, None), P(col + row, None)),
        check_vma=False,
    )
```

```python
import jax
import jax.numpy as jnp
from jax import lax
from jax.experimental import pallas as pl
from jax.experimental.pallas import tpu as pltpu
from jax.sharding import Mesh, PartitionSpec as P

BF, F32 = jnp.bfloat16, jnp.float32
SMEM = pl.BlockSpec(memory_space=pltpu.SMEM)
PARAMS = pltpu.CompilerParams(vmem_limit_bytes=56 * 1024 * 1024)


def split(v):
    hi = v.astype(BF)
    return hi, (v - hi.astype(F32)).astype(BF)


def deal_kernel(search_ref, out_ref):
    part = out_ref.shape[-1]
    for zi in range(out_ref.shape[0]):
        for ci in range(out_ref.shape[1]):
            out_ref[zi, ci] = search_ref[:, ci * part : (ci + 1) * part]


def split_kernel(place_ref, bounds_ref, mine_ref, theirs_ref, out_ref, scalars_ref):
    rows, cols = mine_ref.shape
    core = place_ref[0]
    center = (bounds_ref[2] + bounds_ref[1]) / 2.0
    row = lax.broadcasted_iota(jnp.int32, (rows, cols), 0)
    col = lax.broadcasted_iota(jnp.int32, (rows, cols), 1)
    apart = col - row
    for block, tile_ref in ((core, mine_ref), (1 - core, theirs_ref)):
        offset = place_ref[1] + pl.program_id(0) * rows - block * cols
        hi, lo = split(tile_ref[...] - jnp.where(apart == offset, center, 0.0))
        out_ref[block, 0] = hi
        out_ref[block, 1] = lo

    @pl.when(pl.program_id(0) == 0)
    def _():
        lower, low_end, high_end = (jnp.full((1, scalars_ref.shape[1]), bounds_ref[i], F32) for i in range(3))
        center = (high_end + low_end) / 2.0
        half = (high_end - low_end) / 2.0
        sigma_one = half / (lower - center)
        sigma_two = 1.0 / (2.0 / sigma_one - sigma_one)
        scalars_ref[0:1] = sigma_one / half
        scalars_ref[1:2] = 2.0 * sigma_two / half
        scalars_ref[2:3] = sigma_two * sigma_one


def split_tiles(place, bounds, mine, theirs, width, step=256):
    rows, cols = mine.shape
    tile = pl.BlockSpec((step, cols), lambda i: (i, 0))
    out = pl.BlockSpec((2, 2, step, cols), lambda i: (0, 0, i, 0))
    return pl.pallas_call(
        split_kernel,
        grid=(rows // step,),
        in_specs=[SMEM, SMEM, tile, tile],
        out_specs=(out, pl.BlockSpec((8, width), lambda i: (0, 0))),
        out_shape=(
            jax.ShapeDtypeStruct((2, 2, rows, cols), BF),
            jax.ShapeDtypeStruct((8, width), F32),
        ),
        compiler_params=PARAMS,
        cost_estimate=pl.CostEstimate(flops=16 * rows * cols, bytes_accessed=16 * rows * cols, transcendentals=0),
    )(place, bounds, mine, theirs)


def rows_kernel(h_ref, x_ref, out_ref, wide):
    xs, zc, piece, part = x_ref.shape

    @pl.when(pl.program_id(0) == 0)
    def _():
        for zi in range(zc // 2):
            for block in range(2):
                for xi in range(xs):
                    hi, lo = split(x_ref[xi, zi * 2 + block])
                    at = pl.ds((zi * xs + xi) * piece, piece)
                    wide[block, at, :part] = hi
                    wide[block, at, part:] = lo

    step, cols = h_ref.shape[2:]
    acc = jnp.dot(h_ref[0].reshape(2 * step, cols), wide[0], preferred_element_type=F32)
    acc += jnp.dot(h_ref[1].reshape(2 * step, cols), wide[1], preferred_element_type=F32)
    acc = acc[:, :part] + acc[:, part:]
    out_ref[...] = acc[:step] + acc[step:]


def rows_product(h, x, step=384):
    _, _, rows, cols = h.shape
    xs, zc, piece, part = x.shape
    return pl.pallas_call(
        rows_kernel,
        grid=(rows // step,),
        in_specs=[
            pl.BlockSpec((2, 2, step, cols), lambda i: (0, 0, i, 0)),
            pl.BlockSpec(x.shape, lambda i: (0, 0, 0, 0)),
        ],
        out_specs=pl.BlockSpec((step, part), lambda i: (i, 0)),
        out_shape=jax.ShapeDtypeStruct((rows, part), F32),
        scratch_shapes=[pltpu.VMEM((2, cols, 2 * part), BF)],
        compiler_params=PARAMS,
        cost_estimate=pl.CostEstimate(
            flops=16 * rows * cols * part, bytes_accessed=8 * rows * cols, transcendentals=0
        ),
    )(h, x)


def cols_kernel(h_ref, y_ref, out_ref, tall):
    xs, zs, _, piece, part = out_ref.shape

    @pl.when((pl.program_id(0) == 0) & (pl.program_id(1) == 0))
    def _():
        share = y_ref.shape[1]
        flat = y_ref[...].reshape(y_ref.shape[0] * share, part).T
        hi, lo = split(flat)
        tall[:part] = hi
        tall[part:] = lo

    acc = jnp.dot(tall[...], h_ref[0, 0], preferred_element_type=F32)
    acc += jnp.dot(tall[...], h_ref[0, 1], preferred_element_type=F32)
    out = (acc[:part] + acc[part:]).T
    for zi in range(zs):
        for xi in range(xs):
            at = (zi * xs + xi) * piece
            out_ref[xi, zi, 0] = out[at : at + piece]


def cols_product(h, y, xs, zs, steps=1):
    _, _, rows, cols = h.shape
    part = y.shape[-1]
    piece = cols // (xs * zs)
    return pl.pallas_call(
        cols_kernel,
        grid=(2, steps),
        in_specs=[
            pl.BlockSpec((1, 2, rows, cols // steps), lambda b, j: (b, 0, 0, j)),
            pl.BlockSpec(y.shape, lambda b, j: (0, 0, 0)),
        ],
        out_specs=pl.BlockSpec((xs, zs // steps, 1, piece, part), lambda b, j: (0, j, b, 0, 0)),
        out_shape=jax.ShapeDtypeStruct((xs, zs, 2, piece, part), F32),
        scratch_shapes=[pltpu.VMEM((2 * part, rows), BF)],
        compiler_params=PARAMS,
        cost_estimate=pl.CostEstimate(
            flops=16 * rows * cols * part, bytes_accessed=8 * rows * cols, transcendentals=0
        ),
    )(h, y)


def body(hamiltonian, search_block, filter_bounds):
    z2s, z1s, xs, ys, cs = (lax.axis_size(a) for a in ("z2", "z1", "x", "y", "c"))
    z2, z1, x, y, c = (lax.axis_index(a) for a in ("z2", "z1", "x", "y", "c"))
    rows_tile, cols_tile = hamiltonian.shape
    piece, width = search_block.shape
    part = width // cs
    outer = z1s * xs
    swap = [(i, cs - 1 - i) for i in range(cs)]

    first_row = ((z2 * z1s + z1) * xs + x) * rows_tile
    first_col = y * cs * cols_tile
    other = lax.ppermute(hamiltonian, "c", swap)
    place = jnp.stack([c, first_row - first_col]).astype(jnp.int32)
    tiles, scalars = split_tiles(place, filter_bounds, hamiltonian, other, width)

    sent = pl.pallas_call(deal_kernel, out_shape=jax.ShapeDtypeStruct((z2s, cs, piece, part), F32))(search_block)
    got = lax.all_to_all(sent.reshape(z2s * cs, piece, part), ("z2", "c"), 0, 0, tiled=True)
    got, tiles, scalars = lax.optimization_barrier((got, tiles, scalars))
    scale_one, scale_two, damp = scalars[0, :part], scalars[1, :part], scalars[2]
    sent = jnp.broadcast_to(got[None], (outer,) + got.shape)
    got = lax.all_to_all(sent, ("z1", "x"), 0, 0, tiled=True)

    partial_rows = rows_product(tiles, got)
    share = rows_tile // ys
    terms = lax.all_to_all(partial_rows.reshape(ys, share, part), "y", 0, 0, tiled=True)
    first = scale_one * terms.sum(0)
    sent = jnp.broadcast_to(first[None], terms.shape)
    first_rows = lax.all_to_all(sent, "y", 0, 0, tiled=True)

    first_pair = first.reshape(cs, piece, part)
    keep = lax.dynamic_index_in_dim(first_pair, c, 0, keepdims=False)
    give = lax.dynamic_index_in_dim(first_pair, cs - 1 - c, 0, keepdims=False)
    came = lax.ppermute(give, "c", swap)
    first_out = jnp.where(c == 0, jnp.concatenate([keep, came], 1), jnp.concatenate([came, keep], 1))

    sent = cols_product(tiles, first_rows, outer, z2s).reshape(outer, z2s * cs, piece, part)
    summed = lax.all_to_all(sent, ("z1", "x"), 0, 0, tiled=True).sum(0)
    summed = lax.all_to_all(summed, ("z2", "c"), 0, 0, tiled=True)
    summed = scale_two * summed.reshape(z2s, cs, piece, part).sum(0)
    second_out = summed.transpose(1, 0, 2).reshape(piece, width) - damp * search_block
    return (first_out, second_out)


def solution(mesh):
    fine = Mesh(mesh.devices.reshape(4, 2, 4, 8, 2), ("z2", "z1", "x", "y", "c"))
    row, col = ("z2", "z1", "x"), ("y", "c")
    return jax.shard_map(
        body,
        mesh=fine,
        in_specs=(P(row, col), P(col + row, None), P()),
        out_specs=(P(row + col, None), P(col + row, None)),
        check_vma=False,
    )
```

```python
import jax
import jax.numpy as jnp
from jax import lax
from jax.experimental import pallas as pl
from jax.experimental.pallas import tpu as pltpu
from jax.sharding import Mesh, PartitionSpec as P

BF, F32 = jnp.bfloat16, jnp.float32
SMEM = pl.BlockSpec(memory_space=pltpu.SMEM)
PARAMS = pltpu.CompilerParams(vmem_limit_bytes=56 * 1024 * 1024)


def split(v):
    hi = v.astype(BF)
    return hi, (v - hi.astype(F32)).astype(BF)


def deal_kernel(search_ref, out_ref):
    part = out_ref.shape[-1]
    for zi in range(out_ref.shape[0]):
        for ci in range(out_ref.shape[1]):
            out_ref[zi, ci] = search_ref[:, ci * part : (ci + 1) * part]


def split_kernel(place_ref, bounds_ref, mine_ref, theirs_ref, out_ref, scalars_ref):
    rows, cols = mine_ref.shape
    core = place_ref[0]
    center = (bounds_ref[2] + bounds_ref[1]) / 2.0
    row = lax.broadcasted_iota(jnp.int32, (rows, cols), 0)
    col = lax.broadcasted_iota(jnp.int32, (rows, cols), 1)
    apart = col - row
    for block, tile_ref in ((core, mine_ref), (1 - core, theirs_ref)):
        offset = place_ref[1] + pl.program_id(0) * rows - block * cols
        hi, lo = split(tile_ref[...] - jnp.where(apart == offset, center, 0.0))
        out_ref[block, 0] = hi
        out_ref[block, 1] = lo

    @pl.when(pl.program_id(0) == 0)
    def _():
        lower, low_end, high_end = (jnp.full((1, scalars_ref.shape[1]), bounds_ref[i], F32) for i in range(3))
        center = (high_end + low_end) / 2.0
        half = (high_end - low_end) / 2.0
        sigma_one = half / (lower - center)
        sigma_two = 1.0 / (2.0 / sigma_one - sigma_one)
        scalars_ref[0:1] = sigma_one / half
        scalars_ref[1:2] = 2.0 * sigma_two / half
        scalars_ref[2:3] = sigma_two * sigma_one


def split_tiles(place, bounds, mine, theirs, width, step=384):
    rows, cols = mine.shape
    tile = pl.BlockSpec((step, cols), lambda i: (i, 0))
    out = pl.BlockSpec((2, 2, step, cols), lambda i: (0, 0, i, 0))
    return pl.pallas_call(
        split_kernel,
        grid=(rows // step,),
        in_specs=[SMEM, SMEM, tile, tile],
        out_specs=(out, pl.BlockSpec((8, width), lambda i: (0, 0))),
        out_shape=(
            jax.ShapeDtypeStruct((2, 2, rows, cols), BF),
            jax.ShapeDtypeStruct((8, width), F32),
        ),
        compiler_params=PARAMS,
        cost_estimate=pl.CostEstimate(flops=16 * rows * cols, bytes_accessed=16 * rows * cols, transcendentals=0),
    )(place, bounds, mine, theirs)


def rows_kernel(h_ref, x_ref, out_ref, wide):
    xs, zc, piece, part = x_ref.shape

    @pl.when(pl.program_id(0) == 0)
    def _():
        for zi in range(zc // 2):
            for block in range(2):
                for xi in range(xs):
                    hi, lo = split(x_ref[xi, zi * 2 + block])
                    at = pl.ds((zi * xs + xi) * piece, piece)
                    wide[block, at, :part] = hi
                    wide[block, at, part:] = lo

    step, cols = h_ref.shape[2:]
    acc = jnp.dot(h_ref[0].reshape(2 * step, cols), wide[0], preferred_element_type=F32)
    acc += jnp.dot(h_ref[1].reshape(2 * step, cols), wide[1], preferred_element_type=F32)
    acc = acc[:, :part] + acc[:, part:]
    out_ref[...] = acc[:step] + acc[step:]


def rows_product(h, x, step=384):
    _, _, rows, cols = h.shape
    xs, zc, piece, part = x.shape
    return pl.pallas_call(
        rows_kernel,
        grid=(rows // step,),
        in_specs=[
            pl.BlockSpec((2, 2, step, cols), lambda i: (0, 0, i, 0)),
            pl.BlockSpec(x.shape, lambda i: (0, 0, 0, 0)),
        ],
        out_specs=pl.BlockSpec((step, part), lambda i: (i, 0)),
        out_shape=jax.ShapeDtypeStruct((rows, part), F32),
        scratch_shapes=[pltpu.VMEM((2, cols, 2 * part), BF)],
        compiler_params=PARAMS,
        cost_estimate=pl.CostEstimate(
            flops=16 * rows * cols * part, bytes_accessed=8 * rows * cols, transcendentals=0
        ),
    )(h, x)


def cols_kernel(h_ref, y_ref, out_ref, tall):
    xs, zs, _, piece, part = out_ref.shape

    @pl.when((pl.program_id(0) == 0) & (pl.program_id(1) == 0))
    def _():
        share = y_ref.shape[1]
        flat = y_ref[...].reshape(y_ref.shape[0] * share, part).T
        hi, lo = split(flat)
        tall[:part] = hi
        tall[part:] = lo

    acc = jnp.dot(tall[...], h_ref[0, 0], preferred_element_type=F32)
    acc += jnp.dot(tall[...], h_ref[0, 1], preferred_element_type=F32)
    out = (acc[:part] + acc[part:]).T
    for zi in range(zs):
        for xi in range(xs):
            at = (zi * xs + xi) * piece
            out_ref[xi, zi, 0] = out[at : at + piece]


def cols_product(h, y, xs, zs, steps=1):
    _, _, rows, cols = h.shape
    part = y.shape[-1]
    piece = cols // (xs * zs)
    return pl.pallas_call(
        cols_kernel,
        grid=(2, steps),
        in_specs=[
            pl.BlockSpec((1, 2, rows, cols // steps), lambda b, j: (b, 0, 0, j)),
            pl.BlockSpec(y.shape, lambda b, j: (0, 0, 0)),
        ],
        out_specs=pl.BlockSpec((xs, zs // steps, 1, piece, part), lambda b, j: (0, j, b, 0, 0)),
        out_shape=jax.ShapeDtypeStruct((xs, zs, 2, piece, part), F32),
        scratch_shapes=[pltpu.VMEM((2 * part, rows), BF)],
        compiler_params=PARAMS,
        cost_estimate=pl.CostEstimate(
            flops=16 * rows * cols * part, bytes_accessed=8 * rows * cols, transcendentals=0
        ),
    )(h, y)


def body(hamiltonian, search_block, filter_bounds):
    z2s, z1s, xs, ys, cs = (lax.axis_size(a) for a in ("z2", "z1", "x", "y", "c"))
    z2, z1, x, y, c = (lax.axis_index(a) for a in ("z2", "z1", "x", "y", "c"))
    rows_tile, cols_tile = hamiltonian.shape
    piece, width = search_block.shape
    part = width // cs
    outer = z1s * xs
    swap = [(i, cs - 1 - i) for i in range(cs)]

    first_row = ((z2 * z1s + z1) * xs + x) * rows_tile
    first_col = y * cs * cols_tile
    other = lax.ppermute(hamiltonian, "c", swap)
    place = jnp.stack([c, first_row - first_col]).astype(jnp.int32)
    tiles, scalars = split_tiles(place, filter_bounds, hamiltonian, other, width)

    sent = pl.pallas_call(deal_kernel, out_shape=jax.ShapeDtypeStruct((z2s, cs, piece, part), F32))(search_block)
    got = lax.all_to_all(sent.reshape(z2s * cs, piece, part), ("z2", "c"), 0, 0, tiled=True)
    got, tiles, scalars = lax.optimization_barrier((got, tiles, scalars))
    scale_one, scale_two, damp = scalars[0, :part], scalars[1, :part], scalars[2]
    sent = jnp.broadcast_to(got[None], (outer,) + got.shape)
    got = lax.all_to_all(sent, ("z1", "x"), 0, 0, tiled=True)

    partial_rows = rows_product(tiles, got)
    share = rows_tile // ys
    terms = lax.all_to_all(partial_rows.reshape(ys, share, part), "y", 0, 0, tiled=True)
    first = scale_one * terms.sum(0)
    sent = jnp.broadcast_to(first[None], terms.shape)
    first_rows = lax.all_to_all(sent, "y", 0, 0, tiled=True)

    first_pair = first.reshape(cs, piece, part)
    keep = lax.dynamic_index_in_dim(first_pair, c, 0, keepdims=False)
    give = lax.dynamic_index_in_dim(first_pair, cs - 1 - c, 0, keepdims=False)
    came = lax.ppermute(give, "c", swap)
    first_out = jnp.where(c == 0, jnp.concatenate([keep, came], 1), jnp.concatenate([came, keep], 1))

    sent = cols_product(tiles, first_rows, outer, z2s).reshape(outer, z2s * cs, piece, part)
    summed = lax.all_to_all(sent, ("z1", "x"), 0, 0, tiled=True).sum(0)
    summed = lax.all_to_all(summed, ("z2", "c"), 0, 0, tiled=True)
    summed = scale_two * summed.reshape(z2s, cs, piece, part).sum(0)
    second_out = summed.transpose(1, 0, 2).reshape(piece, width) - damp * search_block
    return (first_out, second_out)


def solution(mesh):
    fine = Mesh(mesh.devices.reshape(4, 2, 4, 8, 2), ("z2", "z1", "x", "y", "c"))
    row, col = ("z2", "z1", "x"), ("y", "c")
    return jax.shard_map(
        body,
        mesh=fine,
        in_specs=(P(row, col), P(col + row, None), P()),
        out_specs=(P(row + col, None), P(col + row, None)),
        check_vma=False,
    )
```

```python
import jax
import jax.numpy as jnp
from jax import lax
from jax.experimental import pallas as pl
from jax.experimental.pallas import tpu as pltpu
from jax.sharding import Mesh, PartitionSpec as P

BF, F32 = jnp.bfloat16, jnp.float32
SMEM = pl.BlockSpec(memory_space=pltpu.SMEM)
PARAMS = pltpu.CompilerParams(vmem_limit_bytes=56 * 1024 * 1024)


def split(v):
    hi = v.astype(BF)
    return hi, (v - hi.astype(F32)).astype(BF)


def deal_kernel(search_ref, out_ref):
    part = out_ref.shape[-1]
    for zi in range(out_ref.shape[0]):
        for ci in range(out_ref.shape[1]):
            out_ref[zi, ci] = search_ref[:, ci * part : (ci + 1) * part]


def split_kernel(place_ref, bounds_ref, mine_ref, theirs_ref, out_ref, scalars_ref):
    rows, cols = mine_ref.shape
    core = place_ref[0]
    center = (bounds_ref[2] + bounds_ref[1]) / 2.0
    row = lax.broadcasted_iota(jnp.int32, (rows, cols), 0)
    col = lax.broadcasted_iota(jnp.int32, (rows, cols), 1)
    apart = col - row
    for block, tile_ref in ((core, mine_ref), (1 - core, theirs_ref)):
        offset = place_ref[1] + pl.program_id(0) * rows - block * cols
        hi, lo = split(tile_ref[...] - jnp.where(apart == offset, center, 0.0))
        out_ref[block, 0] = hi
        out_ref[block, 1] = lo

    @pl.when(pl.program_id(0) == 0)
    def _():
        lower, low_end, high_end = (jnp.full((1, scalars_ref.shape[1]), bounds_ref[i], F32) for i in range(3))
        center = (high_end + low_end) / 2.0
        half = (high_end - low_end) / 2.0
        sigma_one = half / (lower - center)
        sigma_two = 1.0 / (2.0 / sigma_one - sigma_one)
        scalars_ref[0:1] = sigma_one / half
        scalars_ref[1:2] = 2.0 * sigma_two / half
        scalars_ref[2:3] = sigma_two * sigma_one


def split_tiles(place, bounds, mine, theirs, width, step=384):
    rows, cols = mine.shape
    tile = pl.BlockSpec((step, cols), lambda i: (i, 0))
    out = pl.BlockSpec((2, 2, step, cols), lambda i: (0, 0, i, 0))
    return pl.pallas_call(
        split_kernel,
        grid=(rows // step,),
        in_specs=[SMEM, SMEM, tile, tile],
        out_specs=(out, pl.BlockSpec((8, width), lambda i: (0, 0))),
        out_shape=(
            jax.ShapeDtypeStruct((2, 2, rows, cols), BF),
            jax.ShapeDtypeStruct((8, width), F32),
        ),
        compiler_params=PARAMS,
        cost_estimate=pl.CostEstimate(flops=16 * rows * cols, bytes_accessed=16 * rows * cols, transcendentals=0),
    )(place, bounds, mine, theirs)


def rows_kernel(h_ref, x_ref, out_ref, wide):
    xs, zc, piece, part = x_ref.shape

    @pl.when(pl.program_id(0) == 0)
    def _():
        for zi in range(zc // 2):
            for block in range(2):
                for xi in range(xs):
                    hi, lo = split(x_ref[xi, zi * 2 + block])
                    at = pl.ds((zi * xs + xi) * piece, piece)
                    wide[block, at, :part] = hi
                    wide[block, at, part:] = lo

    step, cols = h_ref.shape[2:]
    acc = jnp.dot(h_ref[0].reshape(2 * step, cols), wide[0], preferred_element_type=F32)
    acc += jnp.dot(h_ref[1].reshape(2 * step, cols), wide[1], preferred_element_type=F32)
    acc = acc[:, :part] + acc[:, part:]
    out_ref[...] = acc[:step] + acc[step:]


def rows_product(h, x, step=384):
    _, _, rows, cols = h.shape
    xs, zc, piece, part = x.shape
    return pl.pallas_call(
        rows_kernel,
        grid=(rows // step,),
        in_specs=[
            pl.BlockSpec((2, 2, step, cols), lambda i: (0, 0, i, 0)),
            pl.BlockSpec(x.shape, lambda i: (0, 0, 0, 0)),
        ],
        out_specs=pl.BlockSpec((step, part), lambda i: (i, 0)),
        out_shape=jax.ShapeDtypeStruct((rows, part), F32),
        scratch_shapes=[pltpu.VMEM((2, cols, 2 * part), BF)],
        compiler_params=PARAMS,
        cost_estimate=pl.CostEstimate(
            flops=16 * rows * cols * part, bytes_accessed=8 * rows * cols, transcendentals=0
        ),
    )(h, x)


def cols_kernel(h_ref, y_ref, out_ref, tall):
    xs, zs, _, piece, part = out_ref.shape

    @pl.when((pl.program_id(0) == 0) & (pl.program_id(1) == 0))
    def _():
        share = y_ref.shape[1]
        flat = y_ref[...].reshape(y_ref.shape[0] * share, part).T
        hi, lo = split(flat)
        tall[:part] = hi
        tall[part:] = lo

    acc = jnp.dot(tall[...], h_ref[0, 0], preferred_element_type=F32)
    acc += jnp.dot(tall[...], h_ref[0, 1], preferred_element_type=F32)
    out = (acc[:part] + acc[part:]).T
    for zi in range(zs):
        for xi in range(xs):
            at = (zi * xs + xi) * piece
            out_ref[xi, zi, 0] = out[at : at + piece]


def cols_product(h, y, xs, zs, steps=1):
    _, _, rows, cols = h.shape
    part = y.shape[-1]
    piece = cols // (xs * zs)
    return pl.pallas_call(
        cols_kernel,
        grid=(2, steps),
        in_specs=[
            pl.BlockSpec((1, 2, rows, cols // steps), lambda b, j: (b, 0, 0, j)),
            pl.BlockSpec(y.shape, lambda b, j: (0, 0, 0)),
        ],
        out_specs=pl.BlockSpec((xs, zs // steps, 1, piece, part), lambda b, j: (0, j, b, 0, 0)),
        out_shape=jax.ShapeDtypeStruct((xs, zs, 2, piece, part), F32),
        scratch_shapes=[pltpu.VMEM((2 * part, rows), BF)],
        compiler_params=PARAMS,
        cost_estimate=pl.CostEstimate(
            flops=16 * rows * cols * part, bytes_accessed=8 * rows * cols, transcendentals=0
        ),
    )(h, y)


def body(hamiltonian, search_block, filter_bounds):
    z2s, z1s, xs, ys, cs = (lax.axis_size(a) for a in ("z2", "z1", "x", "y", "c"))
    z2, z1, x, y, c = (lax.axis_index(a) for a in ("z2", "z1", "x", "y", "c"))
    rows_tile, cols_tile = hamiltonian.shape
    piece, width = search_block.shape
    part = width // cs
    outer = z1s * xs
    swap = [(i, cs - 1 - i) for i in range(cs)]

    first_row = ((z2 * z1s + z1) * xs + x) * rows_tile
    first_col = y * cs * cols_tile
    sent = pl.pallas_call(deal_kernel, out_shape=jax.ShapeDtypeStruct((z2s, cs, piece, part), F32))(search_block)
    hamiltonian, sent = lax.optimization_barrier((hamiltonian, sent))
    other = lax.ppermute(hamiltonian, "c", swap)
    place = jnp.stack([c, first_row - first_col]).astype(jnp.int32)
    tiles, scalars = split_tiles(place, filter_bounds, hamiltonian, other, width)

    got = lax.all_to_all(sent.reshape(z2s * cs, piece, part), ("z2", "c"), 0, 0, tiled=True)
    got, tiles, scalars = lax.optimization_barrier((got, tiles, scalars))
    scale_one, scale_two, damp = scalars[0, :part], scalars[1, :part], scalars[2]
    sent = jnp.broadcast_to(got[None], (outer,) + got.shape)
    got = lax.all_to_all(sent, ("z1", "x"), 0, 0, tiled=True)

    partial_rows = rows_product(tiles, got)
    share = rows_tile // ys
    terms = lax.all_to_all(partial_rows.reshape(ys, share, part), "y", 0, 0, tiled=True)
    first = scale_one * terms.sum(0)
    sent = jnp.broadcast_to(first[None], terms.shape)
    first_rows = lax.all_to_all(sent, "y", 0, 0, tiled=True)

    first_pair = first.reshape(cs, piece, part)
    keep = lax.dynamic_index_in_dim(first_pair, c, 0, keepdims=False)
    give = lax.dynamic_index_in_dim(first_pair, cs - 1 - c, 0, keepdims=False)
    came = lax.ppermute(give, "c", swap)
    first_out = jnp.where(c == 0, jnp.concatenate([keep, came], 1), jnp.concatenate([came, keep], 1))

    sent = cols_product(tiles, first_rows, outer, z2s).reshape(outer, z2s * cs, piece, part)
    summed = lax.all_to_all(sent, ("z1", "x"), 0, 0, tiled=True).sum(0)
    summed = lax.all_to_all(summed, ("z2", "c"), 0, 0, tiled=True)
    summed = scale_two * summed.reshape(z2s, cs, piece, part).sum(0)
    second_out = summed.transpose(1, 0, 2).reshape(piece, width) - damp * search_block
    return (first_out, second_out)


def solution(mesh):
    fine = Mesh(mesh.devices.reshape(4, 2, 4, 8, 2), ("z2", "z1", "x", "y", "c"))
    row, col = ("z2", "z1", "x"), ("y", "c")
    return jax.shard_map(
        body,
        mesh=fine,
        in_specs=(P(row, col), P(col + row, None), P()),
        out_specs=(P(row + col, None), P(col + row, None)),
        check_vma=False,
    )
```
